512 devices in a mesh: grp: 32 (over z, y_lo, core), row: 16 (over y_hi, x).
Axes of the slice: x: 4, y: 8 (y_hi: 4, y_lo: 2; y = y_hi * 2 + y_lo), z: 8, core: 2. Of those that a mesh axis runs over, the one named last changes fastest.
Arguments:
- amplitudes: bfloat16 [512, 1792], P(('grp', 'row')), may hold values from -6 to 6
- integrals: bfloat16 [1792, 524288], P(None, ('grp', 'row')), may hold values from -0.125 to 0.125
- occ_energy: float32 [512], replicated, may hold values from -3 to -1
- virt_energy: float32 [524288], P('grp'), may hold values from 1 to 4
Outputs:
- new_amplitudes: bfloat16 [512, 524288], P('row', 'grp')
The draws below stay inside these ranges and needn't reach their ends.
All inputs are finite; a program needn't handle non-finite values.
Results may differ from the reference program's by a relative error of at most 0.001.
Values may be sent and summed in bfloat16 or wider, within the bound.
No kernel may reach another device: no remote copies, remote signals or barrier semaphores. Data moves between devices by JAX's collectives and lax.ppermute only.
A program may use at most 64 MiB of HBM per device.

```python
import jax
import jax.numpy as jnp
from jax import lax

CD = 1792
AB_DEV = 1024
OP = 512
AB = 524288
N_GRP = 32
N_ROW = 16


def block_levels(key, shape, pieces, least, high):
    level, own = 1.0, jax.random.fold_in(key, 6)
    for dim, shards_of in pieces:
        steps = jnp.exp(jax.random.uniform(jax.random.fold_in(own, dim), (shards_of,), jnp.float32, least / len(pieces), high / len(pieces)))
        level = level * jnp.repeat(steps, shape[dim] // shards_of).reshape([-1 if axis == dim else 1 for axis in range(len(shape))])
    return level


def bell_draw(key, dims, width, bound, cuts=(), kind=jnp.bfloat16):
    values = jax.random.normal(key, dims, jnp.float32) * width
    if len(cuts) > 0:
        values = block_levels(key, dims, cuts, -0.22, 0.18) * values
    return jnp.clip(values, min=-bound, max=bound).astype(kind)


def setup_inputs(seed: int = 0) -> dict:
    streams_of = jax.random.split(jax.random.key(seed), 5)
    return {
        "amplitudes": bell_draw(streams_of[0], (OP, CD), 1.0, 6.0, ((0, 512),)),
        "integrals": bell_draw(streams_of[1], (CD, AB), CD ** -0.5, 0.125, ((1, 512),)),
        "occ_energy": jnp.clip(jax.random.uniform(streams_of[2], (OP,), jnp.float32, -3.0, -1.0), -3.0, -1.0),
        "virt_energy": jnp.clip(1.0 + 3.0 * jax.random.uniform(streams_of[3], (AB,), jnp.float32) ** block_levels(streams_of[3], (AB,), ((0, 32),), -0.2, 0.2), 1.0, 4.0),
    }


def reference(amplitudes, integrals, occ_energy, virt_energy):
    def block(index):
        start = (index * AB_DEV).astype(jnp.int32)
        columns = lax.dynamic_slice_in_dim(integrals, start, AB_DEV, 1)
        energies = lax.dynamic_slice_in_dim(virt_energy, start, AB_DEV, 0)
        ladder = jnp.dot(amplitudes, columns, preferred_element_type=jnp.float32)
        return (ladder / (energies[None, :] - occ_energy[:, None])).astype(jnp.bfloat16)

    blocks = lax.map(block, jnp.arange(N_GRP * N_ROW, dtype=jnp.int32))
    return blocks.transpose(1, 0, 2).reshape(OP, AB)
```

```python
import jax
import jax.numpy as jnp
from jax import lax
from jax.sharding import Mesh, PartitionSpec as P

FINE = ("z", "yl", "c", "yh", "x")
SIZES = (8, 2, 2, 4, 4)


def spread(value, axes, peers):
    copies = jnp.broadcast_to(value[None], (peers,) + value.shape)
    return lax.all_to_all(copies, axes, split_axis=0, concat_axis=0, tiled=True)


def shards(amplitudes, integrals, occ_energy, virt_energy):
    row = amplitudes.reshape(14, 128)
    plane = spread(row, ("z", "yl", "yh"), 64)
    half = spread(plane, ("x",), 4)
    half = half.reshape(4, 16, 4, 14, 128).transpose(1, 2, 0, 3, 4).reshape(256, 1792)
    other = lax.ppermute(half, "c", [(0, 1), (1, 0)])

    core = lax.axis_index("c")
    member = lax.axis_index(("yh", "x"))
    virt = lax.dynamic_slice_in_dim(virt_energy, member * 1024, 1024, 0)
    occ = occ_energy.reshape(16, 2, 16)

    def update(rows, which):
        ladder = jnp.dot(rows, integrals, preferred_element_type=jnp.float32)
        occ_rows = lax.dynamic_index_in_dim(occ, which, 1, keepdims=False)
        gap = virt[None, None, :] - occ_rows[:, :, None]
        return (ladder.reshape(16, 16, 1024) / gap).astype(jnp.bfloat16)

    pair = jnp.stack([update(half, core), update(other, 1 - core)], axis=1)
    got = lax.all_to_all(
        pair, ("yh", "x"), split_axis=0, concat_axis=0, tiled=True
    )
    first = jnp.where(core == 0, got[:, 0], got[:, 1])
    second = jnp.where(core == 0, got[:, 1], got[:, 0])
    result = jnp.stack([first, second], axis=0)
    return result.transpose(0, 2, 1, 3).reshape(32, 16384)


def solution(mesh):
    fine = Mesh(mesh.devices.reshape(SIZES), FINE)
    return jax.shard_map(
        shards,
        mesh=fine,
        in_specs=(
            P(FINE, None),
            P(None, FINE),
            P(),
            P(("z", "yl", "c")),
        ),
        out_specs=P(("yh", "x"), ("z", "yl", "c")),
        check_vma=False,
    )
```

```python
import functools

import jax
import jax.numpy as jnp
from jax import lax
from jax.experimental import pallas as pl
from jax.experimental.pallas import tpu as pltpu
from jax.sharding import Mesh, PartitionSpec as P

FINE = ("z", "yl", "c", "yh", "x")
SIZES = (8, 2, 2, 4, 4)
TILE = 256


def spread(value, axes, peers):
    copies = jnp.broadcast_to(value[None], (peers,) + value.shape)
    return lax.all_to_all(copies, axes, split_axis=0, concat_axis=0, tiled=True)


def update_kernel(where, rows_ref, integrals_ref, virt_ref, occ_ref, *rest):
    out_ref = rest[-1]
    slot = where[0]
    occ = occ_ref[pl.ds(slot * 256, 256), :]

    @pl.loop(0, 1024 // TILE)
    def _(tile):
        columns = pl.ds(pl.multiple_of(tile * TILE, TILE), TILE)
        ladder = jnp.dot(
            rows_ref[...], integrals_ref[:, columns], preferred_element_type=jnp.float32
        )
        gap = virt_ref[:, columns] - occ
        result = (ladder / gap).astype(jnp.bfloat16)
        out_ref[:, pl.ds(slot, 1), :, columns] = result.reshape(16, 1, 16, TILE)


def update(slot, rows, integrals, virt, occ, into=None):
    vmem = pl.BlockSpec(memory_space=pltpu.VMEM)
    operands = [jnp.reshape(slot, (1,)), rows, integrals, virt, occ]
    specs = [pl.BlockSpec(memory_space=pltpu.SMEM)] + [vmem] * 4
    aliases = {}
    if into is not None:
        aliases = {len(operands): 0}
        operands.append(into)
        specs.append(pl.BlockSpec(memory_space=pl.ANY))
    return pl.pallas_call(
        update_kernel,
        in_specs=specs,
        out_specs=vmem,
        out_shape=jax.ShapeDtypeStruct((16, 2, 16, 1024), jnp.bfloat16),
        input_output_aliases=aliases,
        compiler_params=pltpu.CompilerParams(vmem_limit_bytes=24 << 20),
        cost_estimate=pl.CostEstimate(
            flops=2 * 256 * 1792 * 1024, bytes_accessed=5 << 20, transcendentals=0
        ),
    )(*operands)


def place_kernel(got_ref, out_ref, sems):
    copies = [
        pltpu.make_async_copy(
            got_ref.at[source], out_ref.at[:, pl.ds(source * 1024, 1024)], sems.at[source]
        )
        for source in range(16)
    ]
    for copy in copies:
        copy.start()
    for copy in copies:
        copy.wait()


def place(got):
    return pl.pallas_call(
        place_kernel,
        in_specs=[pl.BlockSpec(memory_space=pltpu.VMEM)],
        out_specs=pl.BlockSpec(memory_space=pl.ANY),
        out_shape=jax.ShapeDtypeStruct((32, 16384), jnp.bfloat16),
        scratch_shapes=[pltpu.SemaphoreType.DMA((16,))],
    )(got)


def shards(amplitudes, integrals, occ_energy, virt_energy):
    core = lax.axis_index("c")
    member = lax.axis_index(("yh", "x"))
    virt = lax.dynamic_slice_in_dim(virt_energy, member * 1024, 1024, 0)[None]
    occ = occ_energy.reshape(16, 2, 16).transpose(1, 0, 2).reshape(512, 1)
    occ = jnp.broadcast_to(occ, (512, TILE))

    row = amplitudes.reshape(14, 128)
    plane = spread(row, ("z", "yl", "yh"), 64)
    half = spread(plane, ("x",), 4)
    half = half.reshape(4, 16, 4, 14, 128).transpose(1, 2, 0, 3, 4).reshape(256, 1792)
    other = lax.ppermute(half, "c", [(0, 1), (1, 0)])

    out = update(core, half, integrals, virt, occ)
    out = update(1 - core, other, integrals, virt, occ, out)
    got = lax.all_to_all(
        out.reshape(16, 32, 1024), ("yh", "x"), split_axis=0, concat_axis=0, tiled=True
    )
    return place(got)


def solution(mesh):
    fine = Mesh(mesh.devices.reshape(SIZES), FINE)
    return jax.shard_map(
        shards,
        mesh=fine,
        in_specs=(
            P(FINE, None),
            P(None, FINE),
            P(),
            P(("z", "yl", "c")),
        ),
        out_specs=P(("yh", "x"), ("z", "yl", "c")),
        check_vma=False,
    )
```

```python
import jax
import jax.numpy as jnp
from jax import lax
from jax.experimental import pallas as pl
from jax.experimental.pallas import tpu as pltpu
from jax.sharding import Mesh, PartitionSpec as P

FINE = ("z", "yl", "c", "yh", "x")
SIZES = (8, 2, 2, 4, 4)
TILE = 512
TILES = 1024 // TILE
DEEP = 256
BANDS = 1792 // DEEP


def spread(value, axes, peers):
    copies = jnp.broadcast_to(value[None], (peers,) + value.shape)
    return lax.all_to_all(copies, axes, split_axis=0, concat_axis=0, tiled=True)


def divide(ladder, virt, occ, tile):
    parts = []
    for part in range(TILE // 128):
        at = tile * (TILE // 128) + part
        gap = virt[at : at + 1] - occ
        parts.append((ladder[:, part * 128 : part * 128 + 128] / gap).astype(jnp.bfloat16))
    return jnp.concatenate(parts, axis=1)


def first_kernel(
    where, rows_ref, integrals_ref, virt_ref, occ_ref, out_ref, held_ref, total, sems
):
    slot, member = where[0], where[1]
    bands = [slice(band * DEEP, (band + 1) * DEEP) for band in range(BANDS)]
    copies = [
        pltpu.make_async_copy(integrals_ref.at[rows], held_ref.at[rows], sems.at[band])
        for band, rows in enumerate(bands)
    ]
    for copy in copies:
        copy.start()
    occ = occ_ref[pl.ds(slot * 256, 256), :]
    virt = virt_ref[pl.ds(member * 8, 8), :]
    for band, rows in enumerate(bands):
        copies[band].wait()
        for tile in range(TILES):
            columns = slice(tile * TILE, (tile + 1) * TILE)
            ladder = jnp.dot(
                rows_ref[:, rows], held_ref[rows, columns], preferred_element_type=jnp.float32
            )
            if band > 0:
                ladder = ladder + total[:, columns]
            if band < BANDS - 1:
                total[:, columns] = ladder
            else:
                result = divide(ladder, virt, occ, tile)
                out_ref[:, pl.ds(slot, 1), :, columns] = result.reshape(16, 1, 16, TILE)


def second_kernel(where, rows_ref, held_ref, virt_ref, occ_ref, into_ref, out_ref):
    del into_ref
    slot, member = 1 - where[0], where[1]
    occ = occ_ref[pl.ds(slot * 256, 256), :]
    virt = virt_ref[pl.ds(member * 8, 8), :]
    for tile in range(TILES):
        columns = slice(tile * TILE, (tile + 1) * TILE)
        ladder = jnp.dot(
            rows_ref[...], held_ref[:, columns], preferred_element_type=jnp.float32
        )
        result = divide(ladder, virt, occ, tile)
        out_ref[:, pl.ds(slot, 1), :, columns] = result.reshape(16, 1, 16, TILE)


VMEM = pl.BlockSpec(memory_space=pltpu.VMEM)
SMEM = pl.BlockSpec(memory_space=pltpu.SMEM)
ANY = pl.BlockSpec(memory_space=pl.ANY)
UPDATED = jax.ShapeDtypeStruct((16, 2, 16, 1024), jnp.bfloat16)
PARAMS = pltpu.CompilerParams(vmem_limit_bytes=48 << 20)
COST = pl.CostEstimate(
    flops=2 * 256 * 1792 * 1024, bytes_accessed=5 << 20, transcendentals=0
)


def update_first(where, rows, integrals, virt, occ):
    return pl.pallas_call(
        first_kernel,
        in_specs=[SMEM, VMEM, ANY, VMEM, VMEM],
        out_specs=(VMEM, VMEM),
        out_shape=(UPDATED, jax.ShapeDtypeStruct((1792, 1024), jnp.bfloat16)),
        scratch_shapes=[pltpu.VMEM((256, 1024), jnp.float32), pltpu.SemaphoreType.DMA((BANDS,))],
        compiler_params=PARAMS,
        cost_estimate=COST,
    )(where, rows, integrals, virt, occ)


def update_second(where, rows, held, virt, occ, into):
    return pl.pallas_call(
        second_kernel,
        in_specs=[SMEM, VMEM, VMEM, VMEM, VMEM, ANY],
        out_specs=VMEM,
        out_shape=UPDATED,
        input_output_aliases={5: 0},
        compiler_params=PARAMS,
        cost_estimate=COST,
    )(where, rows, held, virt, occ, into)


def gather(amplitudes):
    row = amplitudes.reshape(14, 128)
    plane = spread(row, ("z", "yh"), 32)
    half = spread(plane, ("yl", "x"), 8).reshape(2, 4, 8, 4, 14, 128)
    return half.transpose(2, 0, 3, 1, 4, 5).reshape(256, 1792)


def shards(amplitudes, integrals, occ_energy, virt_energy):
    core = lax.axis_index("c")
    member = lax.axis_index(("yh", "x"))
    where = jnp.stack([core, member])
    virt = virt_energy.reshape(128, 128)
    occ = occ_energy.reshape(16, 2, 16).transpose(1, 0, 2).reshape(512, 1)
    occ = jnp.broadcast_to(occ, (512, 128))

    half = gather(amplitudes)
    other = lax.ppermute(half, "c", [(0, 1), (1, 0)])
    out, held = update_first(where, half, integrals, virt, occ)
    out = update_second(where, other, held, virt, occ, out)
    got = lax.all_to_all(
        out.reshape(16, 32, 1024), ("yh", "x"), split_axis=0, concat_axis=0, tiled=True
    )
    return got.transpose(1, 0, 2).reshape(32, 16384)


def solution(mesh):
    fine = Mesh(mesh.devices.reshape(SIZES), FINE)
    return jax.shard_map(
        shards,
        mesh=fine,
        in_specs=(
            P(FINE, None),
            P(None, FINE),
            P(),
            P(("z", "yl", "c")),
        ),
        out_specs=P(("yh", "x"), ("z", "yl", "c")),
        check_vma=False,
    )
```

```python
import jax
import jax.numpy as jnp
from jax import lax
from jax.experimental import pallas as pl
from jax.experimental.pallas import tpu as pltpu
from jax.sharding import Mesh, PartitionSpec as P

FINE = ("z", "yl", "c", "yh", "x")
SIZES = (8, 2, 2, 4, 4)
DEEP = 256
BANDS = 1792 // DEEP


def spread(value, axes, peers):
    copies = jnp.broadcast_to(value[None], (peers,) + value.shape)
    return lax.all_to_all(copies, axes, split_axis=0, concat_axis=0, tiled=True)


def energies(slot, member, virt_ref, occ_ref, inverse_ref):
    occ = occ_ref[:, pl.ds(slot, 1)].reshape(256, 128)
    virt = virt_ref[pl.ds(member * 8, 8), :]
    for part in range(8):
        inverse_ref[:, part * 128 : (part + 1) * 128] = 1.0 / (virt[part : part + 1] - occ)


def first_kernel(
    core_ref,
    member_ref,
    rows_ref,
    integrals_ref,
    virt_ref,
    occ_ref,
    out_ref,
    held_ref,
    other_ref,
    own_ref,
    lines_ref,
    total,
    sems,
):
    slot, member = core_ref[0], member_ref[0]
    bands = [slice(band * DEEP, (band + 1) * DEEP) for band in range(BANDS)]
    copies = [
        pltpu.make_async_copy(integrals_ref.at[rows], held_ref.at[rows], sems.at[band])
        for band, rows in enumerate(bands)
    ]
    for copy in copies:
        copy.start()
    for block in range(4):
        lines = jnp.broadcast_to(occ_ref[block : block + 1, :], (128, 128)).T
        lines_ref[block * 4 : block * 4 + 4] = lines.reshape(4, 2, 16, 128)
    energies(slot, member, virt_ref, lines_ref, own_ref)
    energies(1 - slot, member, virt_ref, lines_ref, other_ref)
    for band, rows in enumerate(bands):
        copies[band].wait()
        ladder = jnp.dot(
            rows_ref[:, rows], held_ref[rows, :], preferred_element_type=jnp.float32
        )
        if band > 0:
            ladder = ladder + total[...]
        if band < BANDS - 1:
            total[...] = ladder
        else:
            result = (ladder * own_ref[...]).astype(jnp.bfloat16)
            out_ref[:, pl.ds(slot, 1)] = result.reshape(16, 1, 16, 1024)


def second_kernel(core_ref, rows_ref, held_ref, inverse_ref, into_ref, out_ref):
    del into_ref
    slot = 1 - core_ref[0]
    ladder = jnp.dot(rows_ref[...], held_ref[...], preferred_element_type=jnp.float32)
    result = (ladder * inverse_ref[...]).astype(jnp.bfloat16)
    out_ref[:, pl.ds(slot, 1)] = result.reshape(16, 1, 16, 1024)


VMEM = pl.BlockSpec(memory_space=pltpu.VMEM)
SMEM = pl.BlockSpec(memory_space=pltpu.SMEM)
ANY = pl.BlockSpec(memory_space=pl.ANY)
UPDATED = jax.ShapeDtypeStruct((16, 2, 16, 1024), jnp.bfloat16)
PARAMS = pltpu.CompilerParams(vmem_limit_bytes=45 << 20)
COST = pl.CostEstimate(
    flops=2 * 256 * 1792 * 1024, bytes_accessed=5 << 20, transcendentals=0
)


def update_first(core, member, rows, integrals, virt, occ):
    denominators = jax.ShapeDtypeStruct((256, 1024), jnp.float32)
    return pl.pallas_call(
        first_kernel,
        in_specs=[SMEM, SMEM, VMEM, ANY, VMEM, VMEM],
        out_specs=(VMEM, VMEM, VMEM),
        out_shape=(UPDATED, jax.ShapeDtypeStruct((1792, 1024), jnp.bfloat16), denominators),
        scratch_shapes=[
            pltpu.VMEM((256, 1024), jnp.float32),
            pltpu.VMEM((16, 2, 16, 128), jnp.float32),
            pltpu.VMEM((256, 1024), jnp.float32),
            pltpu.SemaphoreType.DMA((BANDS,)),
        ],
        compiler_params=PARAMS,
        cost_estimate=COST,
    )(core, member, rows, integrals, virt, occ)


def update_second(core, rows, held, inverse, into):
    return pl.pallas_call(
        second_kernel,
        in_specs=[SMEM, VMEM, VMEM, VMEM, ANY],
        out_specs=VMEM,
        out_shape=UPDATED,
        input_output_aliases={4: 0},
        compiler_params=PARAMS,
        cost_estimate=COST,
    )(core, rows, held, inverse, into)


def gather(amplitudes):
    row = amplitudes.reshape(14, 128)
    plane = spread(row, ("z", "yh"), 32)
    half = spread(plane, ("yl", "x"), 8).reshape(2, 4, 8, 4, 14, 128)
    return half.transpose(2, 0, 3, 1, 4, 5).reshape(256, 1792)


def shards(amplitudes, integrals, occ_energy, virt_energy):
    core = lax.axis_index("c").reshape(1)
    member = lax.axis_index(("yh", "x")).reshape(1)
    virt = virt_energy.reshape(128, 128)
    occ = occ_energy.reshape(4, 128)

    half = gather(amplitudes)
    other = lax.ppermute(half, "c", [(0, 1), (1, 0)])
    out, held, inverse = update_first(core, member, half, integrals, virt, occ)
    out = update_second(core, other, held, inverse, out)
    got = lax.all_to_all(
        out.reshape(16, 32, 1024), ("yh", "x"), split_axis=0, concat_axis=0, tiled=True
    )
    return got.transpose(1, 0, 2).reshape(32, 16384)


def solution(mesh):
    fine = Mesh(mesh.devices.reshape(SIZES), FINE)
    return jax.shard_map(
        shards,
        mesh=fine,
        in_specs=(
            P(FINE, None),
            P(None, FINE),
            P(),
            P(("z", "yl", "c")),
        ),
        out_specs=P(("yh", "x"), ("z", "yl", "c")),
        check_vma=False,
    )
```

```python
import jax
import jax.numpy as jnp
from jax import lax
from jax.experimental import pallas as pl
from jax.experimental.pallas import tpu as pltpu
from jax.sharding import Mesh, PartitionSpec as P

FINE = ("z", "yl", "c", "yh", "x")
SIZES = (8, 2, 2, 4, 4)
DEEP = 256
BANDS = 1792 // DEEP
KEPT = 3


def spread(value, axes, peers):
    copies = jnp.broadcast_to(value[None], (peers,) + value.shape)
    return lax.all_to_all(copies, axes, split_axis=0, concat_axis=0, tiled=True)


def energies(slot, member, virt_ref, occ_ref, inverse_ref):
    occ = occ_ref[:, pl.ds(slot, 1)].reshape(256, 128)
    virt = virt_ref[pl.ds(member * 8, 8), :]
    for part in range(8):
        inverse_ref[:, part * 128 : (part + 1) * 128] = 1.0 / (virt[part : part + 1] - occ)


def keep_kernel(rows_ref, integrals_ref, out_ref, kept_ref):
    del rows_ref, out_ref
    kept_ref[...] = integrals_ref[: KEPT * DEEP]


def first_kernel(
    core_ref,
    member_ref,
    rows_ref,
    kept_ref,
    integrals_ref,
    virt_ref,
    occ_ref,
    out_ref,
    held_ref,
    other_ref,
    own_ref,
    lines_ref,
    total,
    sems,
):
    slot, member = core_ref[0], member_ref[0]
    bands = [slice(band * DEEP, (band + 1) * DEEP) for band in range(BANDS)]
    copies = [
        pltpu.make_async_copy(integrals_ref.at[rows], held_ref.at[rows], sems.at[band])
        for band, rows in enumerate(bands)
        if band >= KEPT
    ]
    for copy in copies:
        copy.start()
    held_ref[: KEPT * DEEP] = kept_ref[...]
    for block in range(4):
        lines = jnp.broadcast_to(occ_ref[block : block + 1, :], (128, 128)).T
        lines_ref[block * 4 : block * 4 + 4] = lines.reshape(4, 2, 16, 128)
    energies(slot, member, virt_ref, lines_ref, own_ref)
    energies(1 - slot, member, virt_ref, lines_ref, other_ref)
    for band, rows in enumerate(bands):
        if band >= KEPT:
            copies[band - KEPT].wait()
        ladder = jnp.dot(
            rows_ref[:, rows], held_ref[rows, :], preferred_element_type=jnp.float32
        )
        if band > 0:
            ladder = ladder + total[...]
        if band < BANDS - 1:
            total[...] = ladder
        else:
            result = (ladder * own_ref[...]).astype(jnp.bfloat16)
            out_ref[:, pl.ds(slot, 1)] = result.reshape(16, 1, 16, 1024)


def second_kernel(core_ref, rows_ref, held_ref, inverse_ref, into_ref, out_ref):
    del into_ref
    slot = 1 - core_ref[0]
    ladder = jnp.dot(rows_ref[...], held_ref[...], preferred_element_type=jnp.float32)
    result = (ladder * inverse_ref[...]).astype(jnp.bfloat16)
    out_ref[:, pl.ds(slot, 1)] = result.reshape(16, 1, 16, 1024)


VMEM = pl.BlockSpec(memory_space=pltpu.VMEM)
SMEM = pl.BlockSpec(memory_space=pltpu.SMEM)
ANY = pl.BlockSpec(memory_space=pl.ANY)
UPDATED = jax.ShapeDtypeStruct((16, 2, 16, 1024), jnp.bfloat16)
PARAMS = pltpu.CompilerParams(vmem_limit_bytes=45 << 20)
COST = pl.CostEstimate(
    flops=2 * 256 * 1792 * 1024, bytes_accessed=5 << 20, transcendentals=0
)


def keep(rows, integrals):
    return pl.pallas_call(
        keep_kernel,
        in_specs=[VMEM, VMEM],
        out_specs=(VMEM, VMEM),
        out_shape=(
            jax.ShapeDtypeStruct(rows.shape, rows.dtype),
            jax.ShapeDtypeStruct((KEPT * DEEP, 1024), integrals.dtype),
        ),
        input_output_aliases={0: 0},
        compiler_params=pltpu.CompilerParams(vmem_limit_bytes=24 << 20),
    )(rows, integrals)


def update_first(core, member, rows, kept, integrals, virt, occ):
    denominators = jax.ShapeDtypeStruct((256, 1024), jnp.float32)
    return pl.pallas_call(
        first_kernel,
        in_specs=[SMEM, SMEM, VMEM, VMEM, ANY, VMEM, VMEM],
        out_specs=(VMEM, VMEM, VMEM),
        out_shape=(UPDATED, jax.ShapeDtypeStruct((1792, 1024), jnp.bfloat16), denominators),
        scratch_shapes=[
            pltpu.VMEM((256, 1024), jnp.float32),
            pltpu.VMEM((16, 2, 16, 128), jnp.float32),
            pltpu.VMEM((256, 1024), jnp.float32),
            pltpu.SemaphoreType.DMA((BANDS,)),
        ],
        compiler_params=PARAMS,
        cost_estimate=COST,
    )(core, member, rows, kept, integrals, virt, occ)


def update_second(core, rows, held, inverse, into):
    return pl.pallas_call(
        second_kernel,
        in_specs=[SMEM, VMEM, VMEM, VMEM, ANY],
        out_specs=VMEM,
        out_shape=UPDATED,
        input_output_aliases={4: 0},
        compiler_params=PARAMS,
        cost_estimate=COST,
    )(core, rows, held, inverse, into)


def gather(amplitudes):
    row = amplitudes.reshape(14, 128)
    plane = spread(row, ("z", "yh"), 32)
    half = spread(plane, ("yl", "x"), 8).reshape(2, 4, 8, 4, 14, 128)
    return half.transpose(2, 0, 3, 1, 4, 5).reshape(256, 1792)


def shards(amplitudes, integrals, occ_energy, virt_energy):
    core = lax.axis_index("c").reshape(1)
    member = lax.axis_index(("yh", "x")).reshape(1)
    virt = virt_energy.reshape(128, 128)
    occ = occ_energy.reshape(4, 128)

    half, kept = keep(gather(amplitudes), integrals)
    other = lax.ppermute(half, "c", [(0, 1), (1, 0)])
    out, held, inverse = update_first(core, member, half, kept, integrals, virt, occ)
    out = update_second(core, other, held, inverse, out)
    got = lax.all_to_all(
        out.reshape(16, 32, 1024), ("yh", "x"), split_axis=0, concat_axis=0, tiled=True
    )
    return got.transpose(1, 0, 2).reshape(32, 16384)


def solution(mesh):
    fine = Mesh(mesh.devices.reshape(SIZES), FINE)
    return jax.shard_map(
        shards,
        mesh=fine,
        in_specs=(
            P(FINE, None),
            P(None, FINE),
            P(),
            P(("z", "yl", "c")),
        ),
        out_specs=P(("yh", "x"), ("z", "yl", "c")),
        check_vma=False,
    )
```

```python
import jax
import jax.numpy as jnp
from jax import lax
from jax.experimental import pallas as pl
from jax.experimental.pallas import tpu as pltpu
from jax.sharding import Mesh, PartitionSpec as P

FINE = ("z", "yl", "c", "yh", "x")
SIZES = (8, 2, 2, 4, 4)
DEEP = 256
BANDS = 1792 // DEEP
KEPT = 3


def spread(value, axes, peers):
    copies = jnp.broadcast_to(value[None], (peers,) + value.shape)
    return lax.all_to_all(copies, axes, split_axis=0, concat_axis=0, tiled=True)


def energies(slot, member, virt_ref, occ_ref, inverse_ref):
    occ = occ_ref[:, pl.ds(slot, 1)].reshape(256, 128)
    virt = virt_ref[pl.ds(member * 8, 8), :]
    for part in range(8):
        inverse_ref[:, part * 128 : (part + 1) * 128] = 1.0 / (virt[part : part + 1] - occ)


def keep_kernel(rows_ref, integrals_ref, out_ref, kept_ref):
    del rows_ref, out_ref
    kept_ref[...] = integrals_ref[: KEPT * DEEP]


def first_kernel(
    core_ref,
    member_ref,
    rows_ref,
    kept_ref,
    integrals_ref,
    virt_ref,
    occ_ref,
    out_ref,
    held_ref,
    other_ref,
    own_ref,
    lines_ref,
    total,
    sems,
):
    slot, member = core_ref[0], member_ref[0]
    bands = [slice(band * DEEP, (band + 1) * DEEP) for band in range(BANDS)]
    copies = [
        pltpu.make_async_copy(integrals_ref.at[rows], held_ref.at[rows], sems.at[band])
        for band, rows in enumerate(bands)
        if band >= KEPT
    ]
    for copy in copies:
        copy.start()
    held_ref[: KEPT * DEEP] = kept_ref[...]
    for block in range(4):
        lines = jnp.broadcast_to(occ_ref[block : block + 1, :], (128, 128)).T
        lines_ref[block * 4 : block * 4 + 4] = lines.reshape(4, 2, 16, 128)
    energies(slot, member, virt_ref, lines_ref, own_ref)
    energies(1 - slot, member, virt_ref, lines_ref, other_ref)
    for band, rows in enumerate(bands):
        if band >= KEPT:
            copies[band - KEPT].wait()
        ladder = jnp.dot(
            rows_ref[:, rows], held_ref[rows, :], preferred_element_type=jnp.float32
        )
        if band > 0:
            ladder = ladder + total[...]
        if band < BANDS - 1:
            total[...] = ladder
        else:
            result = (ladder * own_ref[...]).astype(jnp.bfloat16)
            out_ref[:, pl.ds(slot, 1)] = result.reshape(16, 1, 16, 1024)


def second_kernel(core_ref, rows_ref, held_ref, inverse_ref, into_ref, out_ref):
    del into_ref
    slot = 1 - core_ref[0]
    ladder = jnp.dot(rows_ref[...], held_ref[...], preferred_element_type=jnp.float32)
    result = (ladder * inverse_ref[...]).astype(jnp.bfloat16)
    out_ref[:, pl.ds(slot, 1)] = result.reshape(16, 1, 16, 1024)


VMEM = pl.BlockSpec(memory_space=pltpu.VMEM)
SMEM = pl.BlockSpec(memory_space=pltpu.SMEM)
ANY = pl.BlockSpec(memory_space=pl.ANY)
UPDATED = jax.ShapeDtypeStruct((16, 2, 16, 1024), jnp.bfloat16)
PARAMS = pltpu.CompilerParams(vmem_limit_bytes=45 << 20)
COST = pl.CostEstimate(
    flops=2 * 256 * 1792 * 1024, bytes_accessed=5 << 20, transcendentals=0
)


def keep(rows, integrals):
    return pl.pallas_call(
        keep_kernel,
        in_specs=[VMEM, VMEM],
        out_specs=(VMEM, VMEM),
        out_shape=(
            jax.ShapeDtypeStruct(rows.shape, rows.dtype),
            jax.ShapeDtypeStruct((KEPT * DEEP, 1024), integrals.dtype),
        ),
        input_output_aliases={0: 0},
        compiler_params=pltpu.CompilerParams(vmem_limit_bytes=24 << 20),
    )(rows, integrals)


def update_first(core, member, rows, kept, integrals, virt, occ):
    denominators = jax.ShapeDtypeStruct((256, 1024), jnp.float32)
    return pl.pallas_call(
        first_kernel,
        in_specs=[SMEM, SMEM, VMEM, VMEM, ANY, VMEM, VMEM],
        out_specs=(VMEM, VMEM, VMEM),
        out_shape=(UPDATED, jax.ShapeDtypeStruct((1792, 1024), jnp.bfloat16), denominators),
        scratch_shapes=[
            pltpu.VMEM((256, 1024), jnp.float32),
            pltpu.VMEM((16, 2, 16, 128), jnp.float32),
            pltpu.VMEM((256, 1024), jnp.float32),
            pltpu.SemaphoreType.DMA((BANDS,)),
        ],
        compiler_params=PARAMS,
        cost_estimate=COST,
    )(core, member, rows, kept, integrals, virt, occ)


def update_second(core, rows, held, inverse, into):
    return pl.pallas_call(
        second_kernel,
        in_specs=[SMEM, VMEM, VMEM, VMEM, ANY],
        out_specs=VMEM,
        out_shape=UPDATED,
        input_output_aliases={4: 0},
        compiler_params=PARAMS,
        cost_estimate=COST,
    )(core, rows, held, inverse, into)


def gather(amplitudes):
    row = amplitudes.reshape(14, 128)
    plane = spread(row, ("yh", "z"), 32)
    half = spread(plane, ("yl", "x"), 8).reshape(2, 4, 4, 8, 14, 128)
    return half.transpose(3, 0, 2, 1, 4, 5).reshape(256, 1792)


def shards(amplitudes, integrals, occ_energy, virt_energy):
    core = lax.axis_index("c").reshape(1)
    member = lax.axis_index(("yh", "x")).reshape(1)
    virt = virt_energy.reshape(128, 128)
    occ = occ_energy.reshape(4, 128)

    half, kept = keep(gather(amplitudes), integrals)
    other = lax.ppermute(half, "c", [(0, 1), (1, 0)])
    out, held, inverse = update_first(core, member, half, kept, integrals, virt, occ)
    out = update_second(core, other, held, inverse, out)
    got = lax.all_to_all(
        out.reshape(16, 32, 1024), ("yh", "x"), split_axis=0, concat_axis=0, tiled=True
    )
    return got.transpose(1, 0, 2).reshape(32, 16384)


def solution(mesh):
    fine = Mesh(mesh.devices.reshape(SIZES), FINE)
    return jax.shard_map(
        shards,
        mesh=fine,
        in_specs=(
            P(FINE, None),
            P(None, FINE),
            P(),
            P(("z", "yl", "c")),
        ),
        out_specs=P(("yh", "x"), ("z", "yl", "c")),
        check_vma=False,
    )
```
